32 devices in a mesh: groups: 2 (over x), expert: 16 (over z, y, core).
Axes of the slice: x: 2, y: 2, z: 4, core: 2. Of those that a mesh axis runs over, the one named last changes fastest.
Arguments:
- tokens: bfloat16 [4096, 2048], P(('groups', 'expert')), parts along dimension 0, may hold values from -6 to 6
- grad_out: bfloat16 [4096, 2048], P(('groups', 'expert')), parts along dimension 0, may hold values from -6 to 6
- routes: int32 [4096, 8], P(('groups', 'expert')), parts along dimension 0, may hold values from 0 to 31, all different within a row; in each aligned block of 128 rows (0 to 127, 128 to 255, ...) at most 40 rows name the same one
- combine_weights: float32 [4096, 8], P(('groups', 'expert')), parts along dimension 0, may hold values from 0.05 to 0.5
- w_gate: bfloat16 [32, 2048, 768], P('expert'), may hold values from -0.125 to 0.125
- w_up: bfloat16 [32, 2048, 768], P('expert'), may hold values from -0.125 to 0.125
- w_down: bfloat16 [32, 768, 2048], P('expert'), may hold values from -0.21875 to 0.21875
Outputs:
- combined: bfloat16 [4096, 2048], P(('groups', 'expert')), parts along dimension 0
- grad_tokens: bfloat16 [4096, 2048], P(('groups', 'expert')), parts along dimension 0
- grad_weights: float32 [4096, 8], P(('groups', 'expert')), parts along dimension 0
The draws below stay inside these ranges and needn't reach their ends.
There are 2 independent parts, one for each index of `groups`. The reference program is written for one: setup_inputs(seed, part) draws one part's arguments, and reference() takes and returns one part's arrays. A program takes and returns all parts, laid end to end along the dimension named above; an argument that names none is the same for every part. Nothing has to cross between parts.
Inputs may be any that keep to these rules, and one draw needn't show every extreme that they name: `routes`: each token names 8 different experts. Among the 128 tokens of one device (aligned blocks of rows) no expert is named more than 40 times.
All inputs are finite; a program needn't handle non-finite values.
Results may differ from the reference program's by a relative error of at most 0.0065.
Values may be sent and summed in bfloat16 or wider, within the bound.
A program may use at most 192 MiB of HBM per device.

```python
import math
import jax
import jax.numpy as jnp
import numpy as np
from jax import lax

D = 2048
FF = 768
TOP = 8
TOK_DEV = 128
EXPERTS = 32
TOKENS = 2048
CAP = 40
N_EXPERT = 16


def steps_of(own_key, shape, pieces, low, high):
    factor_of = 1.0
    for dim, parts in pieces:
        steps = jax.random.uniform(jax.random.fold_in(jax.random.fold_in(own_key, 6), dim), (parts,), jnp.float32, low / len(pieces), high / len(pieces))
        factor_of = factor_of * jnp.repeat(jnp.exp(steps), shape[dim] // parts).reshape((-1,) + (1,) * (len(shape) - 1 - dim))
    return factor_of


def assign_block(own_key, own, number, rows, count, top, reach, slope):
    sequence = jax.random.permutation(own_key, count)
    crowded, common = load_shares(count, rows * top, reach, slope, True), load_shares(count, rows * top, reach, slope, False)
    places = jnp.arange(count)

    def named(sizes, offset_by):
        used = int((sizes > 0).sum())
        fixed = max(1, used // 4)
        shifted = fixed + (places - fixed + offset_by * (used - fixed)) % max(1, count - fixed)
        return jnp.zeros((count,), jnp.int32).at[sequence[jnp.where(places < fixed, places, shifted)]].set(jnp.asarray(sizes, jnp.int32))

    sizes = jnp.where(number % 4 == 0, named(crowded, number // 4), named(common, number - number // 4 - 1))
    mixed = jax.random.permutation(jax.random.fold_in(own, 3), count)
    giver, receiver = mixed[0:count // 2 * 2:2], mixed[1:count // 2 * 2:2]
    margin = jnp.minimum(sizes[giver] - 1, reach - sizes[receiver]) // 2
    margin = jnp.where((giver == sequence[0]) | (receiver == sequence[0]) | (sizes[receiver] == 0), 0, jnp.maximum(margin, 0))
    shifted = jax.random.randint(jax.random.fold_in(own, 4), (count // 2,), 0, 1 << 20) % (margin + 1)
    sizes = sizes.at[giver].add(-shifted).at[receiver].add(shifted)
    members = jnp.searchsorted(jnp.cumsum(sizes), jnp.arange(rows * top), side="right").astype(jnp.int32)
    listing = members.reshape(top, rows).T
    listing = listing[jax.random.permutation(jax.random.fold_in(own, 1), rows)]
    offset_by = jax.random.randint(jax.random.fold_in(own, 2), (rows, 1), 0, top)
    return jnp.take_along_axis(listing, (jnp.arange(top)[None, :] + offset_by) % top, axis=1)


def load_shares(count, total, most, slope, full):
    weights = [(1 << 20) // math.isqrt(grade ** slope) + 1 for grade in range(1, count + 1)]
    largest = most if full else min(most, max(-(-total // count), total * weights[0] // sum(weights)))
    least = 1 if total - largest >= count - 1 else 0
    counts, rest = [largest] + [least] * (count - 1), total - largest - least * (count - 1)
    while rest > 0:
        candidates = [i for i in range(1, count) if counts[i] < largest] or [i for i in range(1, count) if counts[i] < most]
        pool, remaining = sum([weights[i] for i in candidates]), rest
        for i in candidates:
            addition = min(most - counts[i], max(1, remaining * weights[i] // pool), rest)
            counts[i] = counts[i] + addition
            rest = rest - addition
    return np.array(counts)


def normal_values(stream_key, dims, width, reach, split=(), kind=jnp.bfloat16):
    array = width * jax.random.normal(stream_key, dims, jnp.float32)
    if split:
        array = array * steps_of(stream_key, dims, split, -0.22, 0.18)
    return jnp.clip(array, -reach, reach).astype(kind)


def setup_inputs(seed: int = 0, part: int = 0) -> dict:
    key_of = jax.random.split(jax.random.key(seed), 8)
    part_keys = jax.random.split(jax.random.fold_in(key_of[7], part), 8)
    tokens = normal_values(part_keys[0], (TOKENS, D), 1.0, 6.0, ((0, 16),))
    grad_out = normal_values(part_keys[1], (TOKENS, D), 1.0, 6.0, ((0, 16),))
    routes_keys = jax.random.split(jax.random.fold_in(part_keys[2], 1), TOKENS // TOK_DEV)
    routes_turns = jax.random.permutation(jax.random.fold_in(part_keys[2], 3), TOKENS // TOK_DEV)
    routes = jax.vmap(lambda own, number: assign_block(jax.random.fold_in(part_keys[2], 2), own, number, TOK_DEV, EXPERTS, TOP, CAP, 2))(routes_keys, routes_turns).reshape((TOKENS, TOP))
    combine_weights = jnp.clip(jnp.exp(math.log(0.5) - 2.3025851 * jax.random.uniform(part_keys[3], (TOKENS, TOP), jnp.float32) ** steps_of(part_keys[3], (TOKENS, TOP), ((0, 16),), -0.2, 0.2)), 0.05, 0.5)
    w_gate = normal_values(key_of[4], (EXPERTS, D, FF), D ** -0.5, 0.125, ((0, 16),))
    w_up = normal_values(key_of[5], (EXPERTS, D, FF), D ** -0.5, 0.125, ((0, 16),))
    w_down = normal_values(key_of[6], (EXPERTS, FF, D), FF ** -0.5, 0.21875, ((0, 16),))
    return {"tokens": tokens, "grad_out": grad_out, "routes": routes, "combine_weights": combine_weights, "w_gate": w_gate, "w_up": w_up, "w_down": w_down}


def expert_block(operands):
    rows_x, rows_grad, gate_matrix, up_matrix, down_matrix = operands
    gate_pre = jnp.dot(rows_x, gate_matrix, preferred_element_type=jnp.float32)
    up_pre = jnp.dot(rows_x, up_matrix, preferred_element_type=jnp.float32)
    squash = jax.nn.sigmoid(gate_pre)
    activated = gate_pre * squash
    hidden = (activated * up_pre).astype(jnp.bfloat16)
    expert_out = jnp.dot(hidden, down_matrix, preferred_element_type=jnp.float32).astype(jnp.bfloat16)
    hidden_grad = jnp.dot(rows_grad, down_matrix.T, preferred_element_type=jnp.float32)
    gate_grad = (hidden_grad * up_pre * squash * (1.0 + gate_pre * (1.0 - squash))).astype(jnp.bfloat16)
    up_grad = (hidden_grad * activated).astype(jnp.bfloat16)
    row_grad = jnp.dot(gate_grad, gate_matrix.T, preferred_element_type=jnp.float32)
    row_grad = row_grad + jnp.dot(up_grad, up_matrix.T, preferred_element_type=jnp.float32)
    return expert_out, row_grad.astype(jnp.bfloat16)


def reference(tokens, grad_out, routes, combine_weights, w_gate, w_up, w_down):
    matches = routes[:, :, None] == jnp.arange(EXPERTS, dtype=jnp.int32)[None, None, :]
    chosen = jnp.any(matches, axis=1).astype(jnp.int32).reshape(N_EXPERT, TOK_DEV, EXPERTS)
    before = (jnp.cumsum(chosen, axis=1, dtype=jnp.int32) - chosen).reshape(TOKENS, EXPERTS)
    position = jnp.sum(jnp.where(matches, before[:, None, :], 0), axis=2).astype(jnp.int32)
    block_id = (jnp.arange(TOKENS, dtype=jnp.int32) // TOK_DEV).astype(jnp.int32)
    slot_of = ((routes * N_EXPERT + block_id[:, None]) * CAP + position).astype(jnp.int32)
    row_ids = jnp.arange(TOKENS * TOP, dtype=jnp.int32)
    owner_row = jnp.full((EXPERTS * N_EXPERT * CAP,), -1, jnp.int32).at[slot_of.reshape(-1)].set(row_ids)
    filled = owner_row >= 0
    safe_row = jnp.where(filled, owner_row, 0).astype(jnp.int32)
    slot_x = jnp.where(filled[:, None], tokens[safe_row // TOP], 0).astype(tokens.dtype)
    grad_rows = (combine_weights[:, :, None] * grad_out[:, None, :].astype(jnp.float32)).astype(jnp.bfloat16)
    grad_rows = grad_rows.reshape(TOKENS * TOP, D)
    slot_grad = jnp.where(filled[:, None], grad_rows[safe_row], 0).astype(grad_rows.dtype)
    slot_x = slot_x.reshape(EXPERTS, N_EXPERT * CAP, D)
    slot_grad = slot_grad.reshape(EXPERTS, N_EXPERT * CAP, D)
    outputs, grads = lax.map(expert_block, (slot_x, slot_grad, w_gate, w_up, w_down))
    out_rows = outputs.reshape(-1, D)[slot_of].astype(jnp.float32)
    grad_back = grads.reshape(-1, D)[slot_of].astype(jnp.float32)
    combined = jnp.sum(combine_weights[:, :, None] * out_rows, axis=1).astype(jnp.bfloat16)
    grad_weights = jnp.sum(grad_out.astype(jnp.float32)[:, None, :] * out_rows, axis=2)
    grad_tokens = jnp.sum(grad_back, axis=1).astype(jnp.bfloat16)
    return combined, grad_tokens, grad_weights
```

```python
import jax
import jax.numpy as jnp
from jax import lax
from jax.sharding import PartitionSpec as P

F32 = jnp.float32
BF16 = jnp.bfloat16


def shards(tokens, grad_out, routes, combine_weights, w_gate, w_up, w_down):
    nodes = lax.axis_size("expert")
    per_node = w_gate.shape[0]
    tok_rows, top_count = routes.shape
    width = tokens.shape[1]
    experts = per_node * nodes
    cap = 5 * tok_rows * top_count // (4 * experts)
    all_x = lax.all_gather(tokens, "expert")
    matches = routes[:, :, None] == jnp.arange(experts, dtype=jnp.int32)[None, None, :]
    dense = jnp.sum(jnp.where(matches, combine_weights[:, :, None], 0.0), axis=1)
    dense = dense.T.reshape(nodes, per_node, tok_rows)
    here = lax.all_to_all(dense, "expert", split_axis=0, concat_axis=0, tiled=True)
    all_g = lax.all_gather(grad_out, "expert")
    named = here > 0.0
    place = jnp.cumsum(named.astype(jnp.int32), axis=2) - 1
    pick = named[:, :, None, :] & (
        place[:, :, None, :] == jnp.arange(cap, dtype=jnp.int32)[None, None, :, None]
    )
    scale = jnp.sum(jnp.where(pick, here[:, :, None, :], 0.0), axis=3)
    scale = scale.transpose(1, 0, 2).reshape(per_node, nodes * cap, 1)
    hot = pick.astype(BF16).reshape(nodes, per_node * cap, tok_rows)

    def compact(rows):
        got = jnp.einsum("nct,ntd->ncd", hot, rows, preferred_element_type=F32).astype(BF16)
        got = got.reshape(nodes, per_node, cap, width).transpose(1, 0, 2, 3)
        return got.reshape(per_node, nodes * cap, width)

    def spread(rows):
        rows = rows.reshape(per_node, nodes, cap, width).transpose(1, 0, 2, 3)
        rows = rows.reshape(nodes, per_node * cap, width)
        got = jnp.einsum("nct,ncd->ntd", hot, rows, preferred_element_type=F32).astype(BF16)
        return lax.psum_scatter(got, "expert", scatter_dimension=0, tiled=False)

    x = compact(all_x)
    gate = jnp.einsum("erd,edf->erf", x, w_gate, preferred_element_type=F32)
    up = jnp.einsum("erd,edf->erf", x, w_up, preferred_element_type=F32)
    squash = jax.nn.sigmoid(gate)
    act = gate * squash
    hidden = act * up
    out = jnp.einsum(
        "erf,efd->erd", (hidden * scale).astype(BF16), w_down, preferred_element_type=F32
    ).astype(BF16)
    combined = spread(out)
    g = compact(all_g)
    pull = jnp.einsum("erd,efd->erf", g, w_down, preferred_element_type=F32)
    dots = jnp.sum(pull * hidden, axis=2).reshape(per_node, nodes, cap).transpose(1, 0, 2)
    dots = jnp.sum(jnp.where(pick, dots[:, :, :, None], 0.0), axis=2)
    back = lax.all_to_all(dots, "expert", split_axis=0, concat_axis=0, tiled=True)
    back = back.reshape(experts, tok_rows).T
    grad_weights = jnp.sum(jnp.where(matches, back[:, None, :], 0.0), axis=2)
    pull = pull * scale
    gate_grad = (pull * up * squash * (1.0 + gate * (1.0 - squash))).astype(BF16)
    up_grad = (pull * act).astype(BF16)
    row_grad = jnp.einsum("erf,edf->erd", gate_grad, w_gate, preferred_element_type=F32)
    row_grad = row_grad + jnp.einsum("erf,edf->erd", up_grad, w_up, preferred_element_type=F32)
    grad_tokens = spread(row_grad.astype(BF16))
    return (combined, grad_tokens, grad_weights)


def solution(mesh):
    rows = P(("groups", "expert"), None)
    held = P("expert", None, None)
    return jax.shard_map(
        shards,
        mesh=mesh,
        in_specs=(rows, rows, rows, rows, held, held, held),
        out_specs=(rows, rows, rows),
        check_vma=False,
    )
```

```python
import jax
import jax.numpy as jnp
import numpy as np
from jax import lax
from jax.sharding import PartitionSpec as P

F32 = jnp.float32
BF16 = jnp.bfloat16


def ring_order(chips):
    if chips == 8:
        return [0, 2, 4, 6, 7, 5, 3, 1]
    return list(range(chips))


def plan(nodes):
    chips = nodes // 2
    order = ring_order(chips)
    at = {chip: i for i, chip in enumerate(order)}

    def moves(step):
        return [
            (order[i] * 2 + c, order[(i + step) % chips] * 2 + c)
            for i in range(chips)
            for c in range(2)
        ]

    swap = [(i, i ^ 1) for i in range(nodes)]
    half = chips // 2
    groups = [[0]] + [[d, chips - d] for d in range(1, half)] + [[half]]
    slots = [(d, k) for group in groups for d in group for k in range(2)]
    table = np.zeros((nodes, nodes), np.int32)
    for me in range(nodes):
        for j, (d, k) in enumerate(slots):
            table[me, j] = order[(at[me // 2] - d) % chips] * 2 + ((me % 2) ^ k)
    inverse = np.argsort(table, axis=1).astype(np.int32)
    return half, groups, moves(1), moves(-1), swap, table, inverse


def shards(tokens, grad_out, routes, combine_weights, w_gate, w_up, w_down):
    nodes = lax.axis_size("expert")
    per_node = w_gate.shape[0]
    tok_rows, top_count = routes.shape
    width = tokens.shape[1]
    experts = per_node * nodes
    cap = 5 * tok_rows * top_count // (4 * experts)
    mid = tok_rows // 2
    half, groups, right, left, swap, table, inverse = plan(nodes)
    me = lax.axis_index("expert")

    def go_right(rows):
        return lax.ppermute(rows, "expert", right)

    def go_left(rows):
        return lax.ppermute(rows, "expert", left)

    def across(rows):
        return lax.ppermute(rows, "expert", swap)

    def gather_ring(own, after=None):
        rings, last = [[own]], None
        from_left, from_right = own, own
        for _ in range(1, half):
            from_left, from_right = go_right(from_left), go_left(from_right)
            rings.append([from_left, from_right])
        last = jnp.concatenate([go_right(from_left[:mid]), go_left(from_right[mid:])], axis=0)
        rings.append([last])
        return rings, (from_left, from_right)

    matches = routes[:, :, None] == jnp.arange(experts, dtype=jnp.int32)[None, None, :]
    dense = jnp.sum(jnp.where(matches, combine_weights[:, :, None], 0.0), axis=1)
    dense = dense.T.reshape(nodes, per_node, tok_rows)
    here = lax.all_to_all(dense, "expert", split_axis=0, concat_axis=0, tiled=True)
    here = here[jnp.asarray(table)[me]]
    named = here > 0.0
    place = jnp.cumsum(named.astype(jnp.int32), axis=2) - 1
    pick = named[:, :, None, :] & (
        place[:, :, None, :] == jnp.arange(cap, dtype=jnp.int32)[None, None, :, None]
    )
    scale = jnp.sum(jnp.where(pick, here[:, :, None, :], 0.0), axis=3)
    scale = scale.transpose(1, 0, 2).reshape(per_node, nodes * cap, 1)
    hot = pick.astype(BF16).reshape(nodes, per_node * cap, tok_rows)

    starts = np.cumsum([0] + [2 * len(group) for group in groups])

    def compact(rings):
        parts = []
        for number, ring in enumerate(rings):
            rows = jnp.stack([r for own in ring for r in (own, across(own))])
            span = slice(int(starts[number]), int(starts[number + 1]))
            got = jnp.einsum("nct,ntd->ncd", hot[span], rows, preferred_element_type=F32)
            got = got.astype(BF16).reshape(-1, per_node, cap, width)
            parts.append(got.transpose(1, 0, 2, 3).reshape(per_node, -1, width))
        return jnp.concatenate(parts, axis=1)

    def spread(rows):
        rows = rows.reshape(per_node, nodes, cap, width)

        def partials(number):
            span = slice(int(starts[number]), int(starts[number + 1]))
            part = rows[:, span].transpose(1, 0, 2, 3).reshape(-1, per_node * cap, width)
            got = jnp.einsum("nct,ncd->ntd", hot[span], part, preferred_element_type=F32)
            return [
                got[2 * i] + across(got[2 * i + 1].astype(BF16)).astype(F32)
                for i in range(len(groups[number]))
            ]

        far = partials(half)[0].astype(BF16)
        to_left, to_right = go_left(far[:mid]), go_right(far[mid:])
        blank = jnp.zeros((tok_rows - mid, width), BF16)
        to_left = jnp.concatenate([to_left, blank], axis=0)
        to_right = jnp.concatenate([blank, to_right], axis=0)
        for number in range(half - 1, 0, -1):
            near, other = partials(number)
            to_left = go_left((near + to_left.astype(F32)).astype(BF16))
            to_right = go_right((other + to_right.astype(F32)).astype(BF16))
        total = partials(0)[0] + to_left.astype(F32) + to_right.astype(F32)
        return total.astype(BF16)

    rings, ends = gather_ring(tokens)
    x = compact(rings)
    grad_out, _ = lax.optimization_barrier((grad_out, ends))
    rings, _ = gather_ring(grad_out)
    gate = jnp.einsum("erd,edf->erf", x, w_gate, preferred_element_type=F32)
    up = jnp.einsum("erd,edf->erf", x, w_up, preferred_element_type=F32)
    squash = jax.nn.sigmoid(gate)
    act = gate * squash
    hidden = act * up
    out = jnp.einsum(
        "erf,efd->erd", (hidden * scale).astype(BF16), w_down, preferred_element_type=F32
    ).astype(BF16)
    combined = spread(out)
    g = compact(rings)
    pull = jnp.einsum("erd,efd->erf", g, w_down, preferred_element_type=F32)
    dots = jnp.sum(pull * hidden, axis=2).reshape(per_node, nodes, cap).transpose(1, 0, 2)
    dots = jnp.sum(jnp.where(pick, dots[:, :, :, None], 0.0), axis=2)
    dots = dots[jnp.asarray(inverse)[me]]
    back = lax.all_to_all(dots, "expert", split_axis=0, concat_axis=0, tiled=True)
    back = back.reshape(experts, tok_rows).T
    grad_weights = jnp.sum(jnp.where(matches, back[:, None, :], 0.0), axis=2)
    pull = pull * scale
    gate_grad = (pull * up * squash * (1.0 + gate * (1.0 - squash))).astype(BF16)
    up_grad = (pull * act).astype(BF16)
    row_grad = jnp.einsum("erf,edf->erd", gate_grad, w_gate, preferred_element_type=F32)
    row_grad = row_grad + jnp.einsum("erf,edf->erd", up_grad, w_up, preferred_element_type=F32)
    grad_tokens = spread(row_grad.astype(BF16))
    return (combined, grad_tokens, grad_weights)


def solution(mesh):
    rows = P(("groups", "expert"), None)
    held = P("expert", None, None)
    return jax.shard_map(
        shards,
        mesh=mesh,
        in_specs=(rows, rows, rows, rows, held, held, held),
        out_specs=(rows, rows, rows),
        check_vma=False,
    )
```

```python
import jax
import jax.numpy as jnp
import numpy as np
from jax import lax
from jax.sharding import PartitionSpec as P

F32 = jnp.float32
BF16 = jnp.bfloat16


def ring_order(chips):
    if chips == 8:
        return [0, 2, 4, 6, 7, 5, 3, 1]
    return list(range(chips))


def plan(nodes):
    chips = nodes // 2
    order = ring_order(chips)
    at = {chip: i for i, chip in enumerate(order)}

    def moves(step):
        return [
            (order[i] * 2 + c, order[(i + step) % chips] * 2 + c)
            for i in range(chips)
            for c in range(2)
        ]

    swap = [(i, i ^ 1) for i in range(nodes)]
    half = chips // 2
    groups = [[0]] + [[d, chips - d] for d in range(1, half)] + [[half]]
    slots = [(d, k) for group in groups for k in range(2) for d in group]
    table = np.zeros((nodes, nodes), np.int32)
    for me in range(nodes):
        for j, (d, k) in enumerate(slots):
            table[me, j] = order[(at[me // 2] - d) % chips] * 2 + ((me % 2) ^ k)
    inverse = np.argsort(table, axis=1).astype(np.int32)
    return half, groups, moves(1), moves(-1), swap, table, inverse


def shards(tokens, grad_out, routes, combine_weights, w_gate, w_up, w_down):
    nodes = lax.axis_size("expert")
    per_node = w_gate.shape[0]
    tok_rows, top_count = routes.shape
    width = tokens.shape[1]
    experts = per_node * nodes
    cap = 5 * tok_rows * top_count // (4 * experts)
    mid = tok_rows // 2
    half, groups, right, left, swap, table, inverse = plan(nodes)
    me = lax.axis_index("expert")

    def go_right(rows):
        return lax.ppermute(rows, "expert", right)

    def go_left(rows):
        return lax.ppermute(rows, "expert", left)

    def across(rows):
        return lax.ppermute(rows, "expert", swap)

    def gather_ring(own):
        rings = [[own]]
        from_left, from_right = own, own
        for _ in range(1, half):
            from_left, from_right = go_right(from_left), go_left(from_right)
            rings.append([from_left, from_right])
        last = jnp.concatenate([go_right(from_left[:mid]), go_left(from_right[mid:])], axis=0)
        rings.append([last])
        return rings, (from_left, from_right)

    matches = routes[:, :, None] == jnp.arange(experts, dtype=jnp.int32)[None, None, :]
    dense = jnp.sum(jnp.where(matches, combine_weights[:, :, None], 0.0), axis=1)
    dense = dense.T.reshape(nodes, per_node, tok_rows)
    here = lax.all_gather(dense, "expert")
    here = lax.dynamic_index_in_dim(here, me, axis=1, keepdims=False)
    here = here[jnp.asarray(table)[me]]
    named = here > 0.0
    place = jnp.cumsum(named.astype(jnp.int32), axis=2) - 1
    pick = named[:, :, None, :] & (
        place[:, :, None, :] == jnp.arange(cap, dtype=jnp.int32)[None, None, :, None]
    )
    scale = jnp.sum(jnp.where(pick, here[:, :, None, :], 0.0), axis=3)
    scale = scale.transpose(1, 0, 2)
    hot = pick.astype(BF16).reshape(nodes, per_node * cap, tok_rows)

    starts = [int(v) for v in np.cumsum([0] + [2 * len(group) for group in groups])]
    cut = half - 1
    chunks = [(cut, half + 1), (0, cut)]

    def compact(rings, chunk):
        parts = []
        for number in range(*chunk):
            ring = rings[number]
            rows = jnp.stack(ring + [across(own) for own in ring])
            span = slice(starts[number], starts[number + 1])
            got = jnp.einsum("nct,ntd->ncd", hot[span], rows, preferred_element_type=F32)
            got = got.astype(BF16).reshape(-1, per_node, cap, width)
            parts.append(got.transpose(1, 0, 2, 3).reshape(per_node, -1, width))
        return jnp.concatenate(parts, axis=1)

    def chunk_scale(chunk):
        part = scale[:, starts[chunk[0]]:starts[chunk[1]]]
        return part.reshape(per_node, -1, 1)

    def forward(x, weight):
        gate = jnp.einsum("erd,edf->erf", x, w_gate, preferred_element_type=F32)
        up = jnp.einsum("erd,edf->erf", x, w_up, preferred_element_type=F32)
        hidden = (gate * jax.nn.sigmoid(gate) * up * weight).astype(BF16)
        out = jnp.einsum("erf,efd->erd", hidden, w_down, preferred_element_type=F32)
        return out.astype(BF16), gate, up

    def backward_hidden(pull, gate, up, weight):
        squash = jax.nn.sigmoid(gate)
        act = gate * squash
        dots = jnp.sum(pull * act * up, axis=2).reshape(per_node, -1, cap)
        pull = pull * weight
        gate_grad = (pull * up * squash * (1.0 + gate * (1.0 - squash))).astype(BF16)
        return dots, gate_grad, (pull * act).astype(BF16)

    def backward_rows(gate_grad, up_grad):
        rows = jnp.einsum("erf,edf->erd", gate_grad, w_gate, preferred_element_type=F32)
        rows = rows + jnp.einsum("erf,edf->erd", up_grad, w_up, preferred_element_type=F32)
        return rows.astype(BF16)

    def one(rows, slot, base):
        part = rows[:, (slot - base) * cap:(slot - base + 1) * cap].reshape(-1, width)
        return jnp.einsum("ct,cd->td", hot[slot], part, preferred_element_type=F32)

    def swapped(rows, base, number):
        count = len(groups[number])
        return [
            across(one(rows, starts[number] + count + i, base).astype(BF16)) for i in range(count)
        ]

    def pieces(rows, chunk):
        base = starts[chunk[0]]
        got = {}
        for number in reversed(range(*chunk)):
            got[number] = (rows, base, swapped(rows, base, number))
        return got

    def own_sum(piece, number, i):
        rows, base, other = piece[number]
        return one(rows, starts[number] + i, base) + other[i].astype(F32)

    def far_step(piece):
        far = own_sum(piece, half, 0).astype(BF16)
        blank = jnp.zeros((tok_rows - mid, width), BF16)
        to_left = jnp.concatenate([go_left(far[:mid]), blank], axis=0)
        to_right = jnp.concatenate([blank, go_right(far[mid:])], axis=0)
        return to_left, to_right

    def ring_sum(piece, number, moving):
        to_left = (own_sum(piece, number, 0) + moving[0].astype(F32)).astype(BF16)
        to_right = (own_sum(piece, number, 1) + moving[1].astype(F32)).astype(BF16)
        return to_left, to_right

    def ring_send(moving):
        return go_left(moving[0]), go_right(moving[1])

    def last_sum(piece, moving):
        total = own_sum(piece, 0, 0) + moving[0].astype(F32) + moving[1].astype(F32)
        return total.astype(BF16)

    tie = lax.optimization_barrier
    far_span, near_span = chunks
    scales = [chunk_scale(chunk) for chunk in chunks]

    rings, ends = gather_ring(tokens)
    near_x = compact(rings, near_span)
    far_x = compact(rings, far_span)
    grad_out, _ = tie((grad_out, ends))
    rings, ends = gather_ring(grad_out)
    near_out, near_gate, near_up = forward(near_x, scales[1])
    far_out, far_gate, far_up = forward(far_x, scales[0])
    far_out, near_out, _ = tie((far_out, near_out, ends))

    piece = pieces(far_out, far_span)
    piece.update(pieces(near_out, near_span))
    moving = far_step(piece)
    far_g = compact(rings, far_span)
    near_g = compact(rings, near_span)

    stages = list(range(half - 1, 0, -1))
    moving = ring_sum(piece, stages[0], moving)
    far_g, near_g, moving = tie((far_g, near_g, moving))
    moving = ring_send(moving)

    pull = jnp.einsum("erd,efd->erf", far_g, w_down, preferred_element_type=F32)
    dots_far, gate_grad, up_grad = backward_hidden(tie(pull), far_gate, far_up, scales[0])
    if len(stages) > 1:
        moving = ring_sum(piece, stages[1], moving)
        gate_grad, up_grad, near_g, moving = tie((gate_grad, up_grad, near_g, moving))
        moving = ring_send(moving)
    far_rows = backward_rows(gate_grad, up_grad)
    pull = tie(jnp.einsum("erd,efd->erf", near_g, w_down, preferred_element_type=F32))
    for number in stages[2:]:
        moving = ring_sum(piece, number, moving)
        far_rows, pull, moving = tie((far_rows, pull, moving))
        moving = ring_send(moving)
    back_piece = pieces(far_rows, far_span)
    dots_near, gate_grad, up_grad = backward_hidden(pull, near_gate, near_up, scales[1])
    back = far_step(back_piece)
    near_rows = backward_rows(gate_grad, up_grad)
    combined = last_sum(piece, moving)
    back_piece.update(pieces(near_rows, near_span))
    for number in stages:
        back = ring_send(ring_sum(back_piece, number, back))
    grad_tokens = last_sum(back_piece, back)

    dots = jnp.concatenate([dots_near, dots_far], axis=1).transpose(1, 0, 2)
    dots = jnp.sum(jnp.where(pick, dots[:, :, :, None], 0.0), axis=2)
    dots = dots[jnp.asarray(inverse)[me]]
    sent = lax.all_gather(dots, "expert")
    sent = lax.dynamic_index_in_dim(sent, me, axis=1, keepdims=False)
    sent = sent.reshape(experts, tok_rows).T
    grad_weights = jnp.sum(jnp.where(matches, sent[:, None, :], 0.0), axis=2)
    return (combined, grad_tokens, grad_weights)


def solution(mesh):
    rows = P(("groups", "expert"), None)
    held = P("expert", None, None)
    return jax.shard_map(
        shards,
        mesh=mesh,
        in_specs=(rows, rows, rows, rows, held, held, held),
        out_specs=(rows, rows, rows),
        check_vma=False,
    )
```

```python
import jax
import jax.numpy as jnp
import numpy as np
from jax import lax
from jax.sharding import PartitionSpec as P

F32 = jnp.float32
BF16 = jnp.bfloat16


def ring_order(chips):
    if chips == 8:
        return [0, 2, 4, 6, 7, 5, 3, 1]
    return list(range(chips))


def plan(nodes):
    chips = nodes // 2
    order = ring_order(chips)
    at = {chip: i for i, chip in enumerate(order)}

    def moves(step):
        return [
            (order[i] * 2 + c, order[(i + step) % chips] * 2 + c)
            for i in range(chips)
            for c in range(2)
        ]

    swap = [(i, i ^ 1) for i in range(nodes)]
    half = chips // 2
    groups = [[0]] + [[d, chips - d] for d in range(1, half)] + [[half]]
    slots = [(d, k) for group in groups for k in range(2) for d in group]
    table = np.zeros((nodes, nodes), np.int32)
    for me in range(nodes):
        for j, (d, k) in enumerate(slots):
            table[me, j] = order[(at[me // 2] - d) % chips] * 2 + ((me % 2) ^ k)
    inverse = np.argsort(table, axis=1).astype(np.int32)
    return half, groups, moves(1), moves(-1), swap, table, inverse


def shards(tokens, grad_out, routes, combine_weights, w_gate, w_up, w_down):
    nodes = lax.axis_size("expert")
    per_node = w_gate.shape[0]
    tok_rows, top_count = routes.shape
    width = tokens.shape[1]
    experts = per_node * nodes
    cap = 5 * tok_rows * top_count // (4 * experts)
    mid = tok_rows // 2
    half, groups, right, left, swap, table, inverse = plan(nodes)
    me = lax.axis_index("expert")

    def go_right(rows):
        return lax.ppermute(rows, "expert", right)

    def go_left(rows):
        return lax.ppermute(rows, "expert", left)

    def across(rows):
        return lax.ppermute(rows, "expert", swap)

    def gather_ring(own):
        rings = [[own]]
        from_left, from_right = own, own
        for _ in range(1, half):
            from_left, from_right = go_right(from_left), go_left(from_right)
            rings.append([from_left, from_right])
        last = jnp.concatenate([go_right(from_left[:mid]), go_left(from_right[mid:])], axis=0)
        rings.append([last])
        return rings, (from_left, from_right)

    matches = routes[:, :, None] == jnp.arange(experts, dtype=jnp.int32)[None, None, :]
    dense = jnp.sum(jnp.where(matches, combine_weights[:, :, None], 0.0), axis=1)
    dense = dense.T.reshape(nodes, per_node, tok_rows)
    here = lax.all_to_all(dense, "expert", split_axis=0, concat_axis=0, tiled=True)
    here = here[jnp.asarray(table)[me]]
    named = here > 0.0
    place = jnp.cumsum(named.astype(jnp.int32), axis=2) - 1
    pick = named[:, :, None, :] & (
        place[:, :, None, :] == jnp.arange(cap, dtype=jnp.int32)[None, None, :, None]
    )
    scale = jnp.sum(jnp.where(pick, here[:, :, None, :], 0.0), axis=3)
    scale = scale.transpose(1, 0, 2)
    hot = pick.astype(BF16).reshape(nodes, per_node * cap, tok_rows)

    starts = [int(v) for v in np.cumsum([0] + [2 * len(group) for group in groups])]
    cut = half - 1
    chunks = [(cut, half + 1), (0, cut)]

    def compact(rings, chunk):
        parts = []
        for number in range(*chunk):
            ring = rings[number]
            rows = jnp.stack(ring + [across(own) for own in ring])
            span = slice(starts[number], starts[number + 1])
            got = jnp.einsum("nct,ntd->ncd", hot[span], rows, preferred_element_type=F32)
            got = got.astype(BF16).reshape(-1, per_node, cap, width)
            parts.append(got.transpose(1, 0, 2, 3).reshape(per_node, -1, width))
        return jnp.concatenate(parts, axis=1)

    def chunk_scale(chunk):
        part = scale[:, starts[chunk[0]]:starts[chunk[1]]]
        return part.reshape(per_node, -1, 1)

    def forward(x, weight):
        gate = jnp.einsum("erd,edf->erf", x, w_gate, preferred_element_type=F32)
        up = jnp.einsum("erd,edf->erf", x, w_up, preferred_element_type=F32)
        hidden = (gate * jax.nn.sigmoid(gate) * up * weight).astype(BF16)
        out = jnp.einsum("erf,efd->erd", hidden, w_down, preferred_element_type=F32)
        return out.astype(BF16), gate, up

    def backward_hidden(pull, gate, up, weight):
        squash = jax.nn.sigmoid(gate)
        act = gate * squash
        dots = jnp.sum(pull * act * up, axis=2).reshape(per_node, -1, cap)
        pull = pull * weight
        gate_grad = (pull * up * squash * (1.0 + gate * (1.0 - squash))).astype(BF16)
        return dots, gate_grad, (pull * act).astype(BF16)

    def backward_rows(gate_grad, up_grad):
        rows = jnp.einsum("erf,edf->erd", gate_grad, w_gate, preferred_element_type=F32)
        rows = rows + jnp.einsum("erf,edf->erd", up_grad, w_up, preferred_element_type=F32)
        return rows.astype(BF16)

    def one(rows, slot, base):
        part = rows[:, (slot - base) * cap:(slot - base + 1) * cap].reshape(-1, width)
        return jnp.einsum("ct,cd->td", hot[slot], part, preferred_element_type=F32)

    def swapped(rows, base, number):
        count = len(groups[number])
        return [
            across(one(rows, starts[number] + count + i, base).astype(BF16)) for i in range(count)
        ]

    def pieces(rows, chunk):
        base = starts[chunk[0]]
        got = {}
        for number in reversed(range(*chunk)):
            got[number] = (rows, base, swapped(rows, base, number))
        return got

    def own_sum(piece, number, i):
        rows, base, other = piece[number]
        return one(rows, starts[number] + i, base) + other[i].astype(F32)

    def far_step(far):
        blank = jnp.zeros((tok_rows - mid, width), BF16)
        to_left = jnp.concatenate([go_left(far[:mid]), blank], axis=0)
        to_right = jnp.concatenate([blank, go_right(far[mid:])], axis=0)
        return to_left, to_right

    def ring_sum(piece, number, moving):
        to_left = (own_sum(piece, number, 0) + moving[0].astype(F32)).astype(BF16)
        to_right = (own_sum(piece, number, 1) + moving[1].astype(F32)).astype(BF16)
        return to_left, to_right

    def ring_send(moving):
        return go_left(moving[0]), go_right(moving[1])

    def last_sum(piece, moving):
        total = own_sum(piece, 0, 0) + moving[0].astype(F32) + moving[1].astype(F32)
        return total.astype(BF16)

    tie = lax.optimization_barrier
    far_span, near_span = chunks
    scales = [chunk_scale(chunk) for chunk in chunks]

    rings, ends = gather_ring(tokens)
    near_x = compact(rings, near_span)
    far_x = compact(rings, far_span)
    grad_out, _ = tie((grad_out, ends))
    rings, ends = gather_ring(grad_out)
    near_out, near_gate, near_up = forward(near_x, scales[1])
    far_out, far_gate, far_up = forward(far_x, scales[0])
    far_out, near_out, _ = tie((far_out, near_out, ends))

    piece = pieces(far_out, far_span)
    piece.update(pieces(near_out, near_span))
    moving = far_step(own_sum(piece, half, 0).astype(BF16))
    far_g = compact(rings, far_span)
    near_g = compact(rings, near_span)

    stages = list(range(half - 1, 0, -1))
    moving = ring_sum(piece, stages[0], moving)
    far_g, near_g, moving = tie((far_g, near_g, moving))
    moving = ring_send(moving)

    pull = jnp.einsum("erd,efd->erf", far_g, w_down, preferred_element_type=F32)
    dots_far, gate_grad, up_grad = backward_hidden(tie(pull), far_gate, far_up, scales[0])
    if len(stages) > 1:
        moving = ring_sum(piece, stages[1], moving)
        gate_grad, up_grad, near_g, moving = tie((gate_grad, up_grad, near_g, moving))
        moving = ring_send(moving)
    far_rows = backward_rows(gate_grad, up_grad)
    pull = tie(jnp.einsum("erd,efd->erf", near_g, w_down, preferred_element_type=F32))
    for number in stages[2:]:
        moving = ring_sum(piece, number, moving)
        far_rows, pull, moving = tie((far_rows, pull, moving))
        moving = ring_send(moving)
    base = starts[far_span[0]]
    sibling = [
        one(far_rows, starts[n] + len(groups[n]) + i, base).astype(BF16)
        for n in (half, half - 1)
        for i in range(len(groups[n]))
    ]
    pull, sibling = tie((pull, sibling))
    sibling = [across(rows) for rows in sibling]
    back_piece = {
        half: (far_rows, base, sibling[:1]),
        half - 1: (far_rows, base, sibling[1:]),
    }
    dots_near, gate_grad, up_grad = backward_hidden(pull, near_gate, near_up, scales[1])
    dots = jnp.concatenate([dots_near, dots_far], axis=1).transpose(1, 0, 2)
    dots = jnp.sum(jnp.where(pick, dots[:, :, :, None], 0.0), axis=2)
    dots = dots[jnp.asarray(inverse)[me]]
    far = own_sum(back_piece, half, 0).astype(BF16)
    gate_grad, up_grad, far, dots = tie((gate_grad, up_grad, far, dots))
    back = far_step(far)
    sent = lax.all_to_all(dots, "expert", split_axis=0, concat_axis=0, tiled=True)
    near_rows = backward_rows(gate_grad, up_grad)
    combined = last_sum(piece, moving)
    sent = sent.reshape(experts, tok_rows).T
    grad_weights = jnp.sum(jnp.where(matches, sent[:, None, :], 0.0), axis=2)
    back_piece.update(pieces(near_rows, near_span))
    for number in stages:
        back = ring_send(ring_sum(back_piece, number, back))
    grad_tokens = last_sum(back_piece, back)

    return (combined, grad_tokens, grad_weights)


def solution(mesh):
    rows = P(("groups", "expert"), None)
    held = P("expert", None, None)
    return jax.shard_map(
        shards,
        mesh=mesh,
        in_specs=(rows, rows, rows, rows, held, held, held),
        out_specs=(rows, rows, rows),
        check_vma=False,
    )
```

```python
import jax
import jax.numpy as jnp
import numpy as np
from jax import lax
from jax.sharding import PartitionSpec as P

F32 = jnp.float32
BF16 = jnp.bfloat16


def ring_order(chips):
    if chips == 8:
        return [0, 2, 4, 6, 7, 5, 3, 1]
    return list(range(chips))


def plan(nodes):
    chips = nodes // 2
    order = ring_order(chips)
    at = {chip: i for i, chip in enumerate(order)}

    def moves(step):
        return [
            (order[i] * 2 + c, order[(i + step) % chips] * 2 + c)
            for i in range(chips)
            for c in range(2)
        ]

    swap = [(i, i ^ 1) for i in range(nodes)]
    half = chips // 2
    groups = [[0]] + [[d, chips - d] for d in range(1, half)] + [[half]]
    slots = [(d, k) for group in groups for k in range(2) for d in group]
    table = np.zeros((nodes, nodes), np.int32)
    for me in range(nodes):
        for j, (d, k) in enumerate(slots):
            table[me, j] = order[(at[me // 2] - d) % chips] * 2 + ((me % 2) ^ k)
    inverse = np.argsort(table, axis=1).astype(np.int32)
    return half, groups, moves(1), moves(-1), swap, table, inverse


def shards(tokens, grad_out, routes, combine_weights, w_gate, w_up, w_down):
    nodes = lax.axis_size("expert")
    per_node = w_gate.shape[0]
    tok_rows, top_count = routes.shape
    width = tokens.shape[1]
    experts = per_node * nodes
    cap = 5 * tok_rows * top_count // (4 * experts)
    mid = tok_rows // 2
    half, groups, right, left, swap, table, inverse = plan(nodes)
    me = lax.axis_index("expert")

    def go_right(rows):
        return lax.ppermute(rows, "expert", right)

    def go_left(rows):
        return lax.ppermute(rows, "expert", left)

    def across(rows):
        return lax.ppermute(rows, "expert", swap)

    def gather_ring(own):
        rings = [[own]]
        from_left, from_right = own, own
        for _ in range(1, half):
            from_left, from_right = go_right(from_left), go_left(from_right)
            rings.append([from_left, from_right])
        last = jnp.concatenate([go_right(from_left[:mid]), go_left(from_right[mid:])], axis=0)
        rings.append([last])
        return rings, (from_left, from_right)

    tie = lax.optimization_barrier
    rings, ends = gather_ring(tokens)
    matches = routes[:, :, None] == jnp.arange(experts, dtype=jnp.int32)[None, None, :]
    dense = jnp.sum(jnp.where(matches, combine_weights[:, :, None], 0.0), axis=1)
    dense = dense.T.reshape(nodes, per_node, tok_rows)
    here = lax.all_to_all(dense, "expert", split_axis=0, concat_axis=0, tiled=True)
    here, _ = tie((here, rings[min(2, half - 1)]))
    here = here[jnp.asarray(table)[me]]
    named = here > 0.0
    place = jnp.cumsum(named.astype(jnp.int32), axis=2) - 1
    pick = named[:, :, None, :] & (
        place[:, :, None, :] == jnp.arange(cap, dtype=jnp.int32)[None, None, :, None]
    )
    scale = jnp.sum(jnp.where(pick, here[:, :, None, :], 0.0), axis=3)
    scale = scale.transpose(1, 0, 2)
    hot = pick.astype(BF16).reshape(nodes, per_node * cap, tok_rows)

    starts = [int(v) for v in np.cumsum([0] + [2 * len(group) for group in groups])]
    cut = half - 1
    chunks = [(cut, half + 1), (0, cut)]

    def compact(rings, chunk):
        parts = []
        for number in range(*chunk):
            ring = rings[number]
            rows = jnp.stack(ring + [across(own) for own in ring])
            span = slice(starts[number], starts[number + 1])
            got = jnp.einsum("nct,ntd->ncd", hot[span], rows, preferred_element_type=F32)
            got = got.astype(BF16).reshape(-1, per_node, cap, width)
            parts.append(got.transpose(1, 0, 2, 3).reshape(per_node, -1, width))
        return jnp.concatenate(parts, axis=1)

    def chunk_scale(chunk):
        part = scale[:, starts[chunk[0]]:starts[chunk[1]]]
        return part.reshape(per_node, -1, 1)

    def forward(x, weight):
        gate = jnp.einsum("erd,edf->erf", x, w_gate, preferred_element_type=F32)
        up = jnp.einsum("erd,edf->erf", x, w_up, preferred_element_type=F32)
        hidden = (gate * jax.nn.sigmoid(gate) * up * weight).astype(BF16)
        out = jnp.einsum("erf,efd->erd", hidden, w_down, preferred_element_type=F32)
        return out.astype(BF16), gate, up

    def backward_hidden(pull, gate, up, weight):
        squash = jax.nn.sigmoid(gate)
        act = gate * squash
        dots = jnp.sum(pull * act * up, axis=2).reshape(per_node, -1, cap)
        pull = pull * weight
        gate_grad = (pull * up * squash * (1.0 + gate * (1.0 - squash))).astype(BF16)
        return dots, gate_grad, (pull * act).astype(BF16)

    def backward_rows(gate_grad, up_grad):
        rows = jnp.einsum("erf,edf->erd", gate_grad, w_gate, preferred_element_type=F32)
        rows = rows + jnp.einsum("erf,edf->erd", up_grad, w_up, preferred_element_type=F32)
        return rows.astype(BF16)

    def one(rows, slot, base):
        part = rows[:, (slot - base) * cap:(slot - base + 1) * cap].reshape(-1, width)
        return jnp.einsum("ct,cd->td", hot[slot], part, preferred_element_type=F32)

    def swapped(rows, base, number):
        count = len(groups[number])
        return [
            across(one(rows, starts[number] + count + i, base).astype(BF16)) for i in range(count)
        ]

    def pieces(rows, chunk):
        base = starts[chunk[0]]
        got = {}
        for number in reversed(range(*chunk)):
            got[number] = (rows, base, swapped(rows, base, number))
        return got

    def own_sum(piece, number, i):
        rows, base, other = piece[number]
        return one(rows, starts[number] + i, base) + other[i].astype(F32)

    def far_step(far):
        blank = jnp.zeros((tok_rows - mid, width), BF16)
        to_left = jnp.concatenate([go_left(far[:mid]), blank], axis=0)
        to_right = jnp.concatenate([blank, go_right(far[mid:])], axis=0)
        return to_left, to_right

    def ring_sum(piece, number, moving):
        to_left = (own_sum(piece, number, 0) + moving[0].astype(F32)).astype(BF16)
        to_right = (own_sum(piece, number, 1) + moving[1].astype(F32)).astype(BF16)
        return to_left, to_right

    def ring_send(moving):
        return go_left(moving[0]), go_right(moving[1])

    def last_sum(piece, moving):
        total = own_sum(piece, 0, 0) + moving[0].astype(F32) + moving[1].astype(F32)
        return total.astype(BF16)

    far_span, near_span = chunks
    scales = [chunk_scale(chunk) for chunk in chunks]

    near_x = compact(rings, near_span)
    far_x = compact(rings, far_span)
    grad_out, _ = tie((grad_out, ends))
    rings, ends = gather_ring(grad_out)
    near_out, near_gate, near_up = forward(near_x, scales[1])
    far_out, far_gate, far_up = forward(far_x, scales[0])
    far_out, near_out, _ = tie((far_out, near_out, ends))

    piece = pieces(far_out, far_span)
    piece.update(pieces(near_out, near_span))
    moving = far_step(own_sum(piece, half, 0).astype(BF16))
    far_g = compact(rings, far_span)
    near_g = compact(rings, near_span)

    stages = list(range(half - 1, 0, -1))
    moving = ring_sum(piece, stages[0], moving)
    far_g, near_g, moving = tie((far_g, near_g, moving))
    moving = ring_send(moving)

    pull = jnp.einsum("erd,efd->erf", far_g, w_down, preferred_element_type=F32)
    dots_far, gate_grad, up_grad = backward_hidden(tie(pull), far_gate, far_up, scales[0])
    if len(stages) > 1:
        moving = ring_sum(piece, stages[1], moving)
        gate_grad, up_grad, near_g, moving = tie((gate_grad, up_grad, near_g, moving))
        moving = ring_send(moving)
    far_rows = backward_rows(gate_grad, up_grad)
    pull = tie(jnp.einsum("erd,efd->erf", near_g, w_down, preferred_element_type=F32))
    for number in stages[2:]:
        moving = ring_sum(piece, number, moving)
        far_rows, pull, moving = tie((far_rows, pull, moving))
        moving = ring_send(moving)
    base = starts[far_span[0]]
    sibling = [
        one(far_rows, starts[n] + len(groups[n]) + i, base).astype(BF16)
        for n in (half, half - 1)
        for i in range(len(groups[n]))
    ]
    pull, sibling = tie((pull, sibling))
    sibling = [across(rows) for rows in sibling]
    back_piece = {
        half: (far_rows, base, sibling[:1]),
        half - 1: (far_rows, base, sibling[1:]),
    }
    dots_near, gate_grad, up_grad = backward_hidden(pull, near_gate, near_up, scales[1])
    dots = jnp.concatenate([dots_near, dots_far], axis=1).transpose(1, 0, 2)
    dots = jnp.sum(jnp.where(pick, dots[:, :, :, None], 0.0), axis=2)
    dots = dots[jnp.asarray(inverse)[me]]
    far = own_sum(back_piece, half, 0).astype(BF16)
    gate_grad, up_grad, far, dots = tie((gate_grad, up_grad, far, dots))
    back = far_step(far)
    sent = lax.all_to_all(dots, "expert", split_axis=0, concat_axis=0, tiled=True)
    near_rows = backward_rows(gate_grad, up_grad)
    combined = last_sum(piece, moving)
    sent = sent.reshape(experts, tok_rows).T
    grad_weights = jnp.sum(jnp.where(matches, sent[:, None, :], 0.0), axis=2)
    back_piece.update(pieces(near_rows, near_span))
    for number in stages:
        if number == 1:
            others = [back_piece[n][2] for n in (0, 1)]
            others, back = tie((others, back))
            for n in (0, 1):
                back_piece[n] = back_piece[n][:2] + (others[n],)
        back = ring_send(ring_sum(back_piece, number, back))
    grad_tokens = last_sum(back_piece, back)

    return (combined, grad_tokens, grad_weights)


def solution(mesh):
    rows = P(("groups", "expert"), None)
    held = P("expert", None, None)
    return jax.shard_map(
        shards,
        mesh=mesh,
        in_specs=(rows, rows, rows, rows, held, held, held),
        out_specs=(rows, rows, rows),
        check_vma=False,
    )
```

```python
import jax
import jax.numpy as jnp
import numpy as np
from jax import lax
from jax.sharding import PartitionSpec as P

F32 = jnp.float32
BF16 = jnp.bfloat16


def ring_order(chips):
    if chips == 8:
        return [0, 2, 4, 6, 7, 5, 3, 1]
    return list(range(chips))


def plan(nodes):
    chips = nodes // 2
    order = ring_order(chips)
    at = {chip: i for i, chip in enumerate(order)}

    def moves(step):
        return [
            (order[i] * 2 + c, order[(i + step) % chips] * 2 + c)
            for i in range(chips)
            for c in range(2)
        ]

    swap = [(i, i ^ 1) for i in range(nodes)]
    half = chips // 2
    groups = [[0]] + [[d, chips - d] for d in range(1, half)] + [[half]]
    slots = [(d, k) for group in groups for k in range(2) for d in group]
    table = np.zeros((nodes, nodes), np.int32)
    for me in range(nodes):
        for j, (d, k) in enumerate(slots):
            table[me, j] = order[(at[me // 2] - d) % chips] * 2 + ((me % 2) ^ k)
    inverse = np.argsort(table, axis=1).astype(np.int32)
    return half, groups, moves(1), moves(-1), swap, table, inverse


def shards(tokens, grad_out, routes, combine_weights, w_gate, w_up, w_down):
    nodes = lax.axis_size("expert")
    per_node = w_gate.shape[0]
    tok_rows, top_count = routes.shape
    width = tokens.shape[1]
    experts = per_node * nodes
    cap = 5 * tok_rows * top_count // (4 * experts)
    mid = tok_rows // 2
    half, groups, right, left, swap, table, inverse = plan(nodes)
    me = lax.axis_index("expert")

    def go_right(rows):
        return lax.ppermute(rows, "expert", right)

    def go_left(rows):
        return lax.ppermute(rows, "expert", left)

    def across(rows):
        return lax.ppermute(rows, "expert", swap)

    def gather_ring(own):
        rings = [[own]]
        from_left, from_right = own, own
        for _ in range(1, half):
            from_left, from_right = go_right(from_left), go_left(from_right)
            rings.append([from_left, from_right])
        last = jnp.concatenate([go_right(from_left[:mid]), go_left(from_right[mid:])], axis=0)
        rings.append([last])
        return rings, (from_left, from_right)

    tie = lax.optimization_barrier
    rings, ends = gather_ring(tokens)
    matches = routes[:, :, None] == jnp.arange(experts, dtype=jnp.int32)[None, None, :]
    dense = jnp.sum(jnp.where(matches, combine_weights[:, :, None], 0.0), axis=1)
    dense = dense.T.reshape(nodes, per_node, tok_rows)
    here = lax.all_to_all(dense, "expert", split_axis=0, concat_axis=0, tiled=True)
    here, _ = tie((here, rings[min(2, half - 1)]))
    here = here[jnp.asarray(table)[me]]
    named = here > 0.0
    place = jnp.cumsum(named.astype(jnp.int32), axis=2) - 1
    pick = named[:, :, None, :] & (
        place[:, :, None, :] == jnp.arange(cap, dtype=jnp.int32)[None, None, :, None]
    )
    scale = jnp.sum(jnp.where(pick, here[:, :, None, :], 0.0), axis=3)
    scale = scale.transpose(1, 0, 2)
    hot = pick.astype(BF16).reshape(nodes, per_node * cap, tok_rows)

    starts = [int(v) for v in np.cumsum([0] + [2 * len(group) for group in groups])]
    cut = half - 1
    chunks = [(cut, half + 1), (0, cut)]

    def compact(rings, chunk):
        parts = []
        for number in range(*chunk):
            ring = rings[number]
            rows = jnp.stack(ring + [across(own) for own in ring])
            span = slice(starts[number], starts[number + 1])
            got = jnp.einsum("nct,ntd->ncd", hot[span], rows, preferred_element_type=F32)
            got = got.astype(BF16).reshape(-1, per_node, cap, width)
            parts.append(got.transpose(1, 0, 2, 3).reshape(per_node, -1, width))
        return jnp.concatenate(parts, axis=1)

    def chunk_scale(chunk):
        part = scale[:, starts[chunk[0]]:starts[chunk[1]]]
        return part.reshape(per_node, -1, 1)

    def forward(x, weight):
        gate = jnp.einsum("erd,edf->erf", x, w_gate, preferred_element_type=F32)
        up = jnp.einsum("erd,edf->erf", x, w_up, preferred_element_type=F32)
        hidden = (gate * jax.nn.sigmoid(gate) * up * weight).astype(BF16)
        out = jnp.einsum("erf,efd->erd", hidden, w_down, preferred_element_type=F32)
        return out.astype(BF16), gate, up

    def backward_hidden(pull, gate, up, weight):
        squash = jax.nn.sigmoid(gate)
        act = gate * squash
        dots = jnp.sum(pull * act * up, axis=2).reshape(per_node, -1, cap)
        pull = pull * weight
        gate_grad = (pull * up * squash * (1.0 + gate * (1.0 - squash))).astype(BF16)
        return dots, gate_grad, (pull * act).astype(BF16)

    def backward_rows(gate_grad, up_grad):
        rows = jnp.einsum("erf,edf->erd", gate_grad, w_gate, preferred_element_type=F32)
        rows = rows + jnp.einsum("erf,edf->erd", up_grad, w_up, preferred_element_type=F32)
        return rows.astype(BF16)

    def one(rows, slot, base):
        part = rows[:, (slot - base) * cap:(slot - base + 1) * cap].reshape(-1, width)
        return jnp.einsum("ct,cd->td", hot[slot], part, preferred_element_type=F32)

    def swapped(rows, base, number):
        count = len(groups[number])
        return [
            across(one(rows, starts[number] + count + i, base).astype(BF16)) for i in range(count)
        ]

    def pieces(rows, chunk):
        base = starts[chunk[0]]
        got = {}
        for number in reversed(range(*chunk)):
            got[number] = (rows, base, swapped(rows, base, number))
        return got

    def own_sum(piece, number, i):
        rows, base, other = piece[number]
        return one(rows, starts[number] + i, base) + other[i].astype(F32)

    def far_step(far):
        blank = jnp.zeros((tok_rows - mid, width), BF16)
        to_left = jnp.concatenate([go_left(far[:mid]), blank], axis=0)
        to_right = jnp.concatenate([blank, go_right(far[mid:])], axis=0)
        return to_left, to_right

    def ring_sum(piece, number, moving):
        to_left = (own_sum(piece, number, 0) + moving[0].astype(F32)).astype(BF16)
        to_right = (own_sum(piece, number, 1) + moving[1].astype(F32)).astype(BF16)
        return to_left, to_right

    def ring_send(moving):
        return go_left(moving[0]), go_right(moving[1])

    def last_sum(piece, moving):
        total = own_sum(piece, 0, 0) + moving[0].astype(F32) + moving[1].astype(F32)
        return total.astype(BF16)

    far_span, near_span = chunks
    scales = [chunk_scale(chunk) for chunk in chunks]

    near_x = compact(rings, near_span)
    far_x = compact(rings, far_span)
    grad_out, _ = tie((grad_out, ends))
    rings, ends = gather_ring(grad_out)
    near_out, near_gate, near_up = forward(near_x, scales[1])
    far_out, far_gate, far_up = forward(far_x, scales[0])
    far_out, near_out, _ = tie((far_out, near_out, ends))

    piece = pieces(far_out, far_span)
    piece.update(pieces(near_out, near_span))
    moving = far_step(own_sum(piece, half, 0).astype(BF16))
    far_g = compact(rings, far_span)
    near_g = compact(rings, near_span)

    stages = list(range(half - 1, 0, -1))
    moving = ring_sum(piece, stages[0], moving)
    far_g, near_g, moving = tie((far_g, near_g, moving))
    moving = ring_send(moving)

    pull = jnp.einsum("erd,efd->erf", far_g, w_down, preferred_element_type=F32)
    dots_far, gate_grad, up_grad = backward_hidden(tie(pull), far_gate, far_up, scales[0])
    if len(stages) > 1:
        moving = ring_sum(piece, stages[1], moving)
        gate_grad, up_grad, near_g, moving = tie((gate_grad, up_grad, near_g, moving))
        moving = ring_send(moving)
    far_rows = backward_rows(gate_grad, up_grad)
    pull = tie(jnp.einsum("erd,efd->erf", near_g, w_down, preferred_element_type=F32))
    for number in stages[2:]:
        moving = ring_sum(piece, number, moving)
        far_rows, pull, moving = tie((far_rows, pull, moving))
        moving = ring_send(moving)
    base = starts[far_span[0]]
    sibling = [
        one(far_rows, starts[n] + len(groups[n]) + i, base).astype(BF16)
        for n in (half, half - 1)
        for i in range(len(groups[n]))
    ]
    pull, sibling = tie((pull, sibling))
    sibling = [across(rows) for rows in sibling]
    back_piece = {
        half: (far_rows, base, sibling[:1]),
        half - 1: (far_rows, base, sibling[1:]),
    }
    dots_near, gate_grad, up_grad = backward_hidden(pull, near_gate, near_up, scales[1])
    dots = jnp.concatenate([dots_near, dots_far], axis=1).transpose(1, 0, 2)
    dots = jnp.sum(jnp.where(pick, dots[:, :, :, None], 0.0), axis=2)
    dots = dots[jnp.asarray(inverse)[me]]
    far = own_sum(back_piece, half, 0).astype(BF16)
    gate_grad, up_grad, far, dots = tie((gate_grad, up_grad, far, dots))
    back = far_step(far)
    sent = lax.all_to_all(dots, "expert", split_axis=0, concat_axis=0, tiled=True)
    near_rows = backward_rows(gate_grad, up_grad)
    near_rows, moving = tie((near_rows, moving))
    combined = last_sum(piece, moving)
    sent = sent.reshape(experts, tok_rows).T
    grad_weights = jnp.sum(jnp.where(matches, sent[:, None, :], 0.0), axis=2)
    back_piece.update(pieces(near_rows, near_span))
    for number in stages:
        if number == 1:
            others = [back_piece[n][2] for n in (0, 1)]
            others, back = tie((others, back))
            for n in (0, 1):
                back_piece[n] = back_piece[n][:2] + (others[n],)
        back = ring_send(ring_sum(back_piece, number, back))
    grad_tokens = last_sum(back_piece, back)

    return (combined, grad_tokens, grad_weights)


def solution(mesh):
    rows = P(("groups", "expert"), None)
    held = P("expert", None, None)
    return jax.shard_map(
        shards,
        mesh=mesh,
        in_specs=(rows, rows, rows, rows, held, held, held),
        out_specs=(rows, rows, rows),
        check_vma=False,
    )
```
